32 devices in a mesh: groups: 2 (over x), req: 16 (over z, y, core).
Axes of the slice: x: 2, y: 2, z: 4, core: 2. Of those that a mesh axis runs over, the one named last changes fastest.
Arguments:
- normed_hidden: bfloat16 [6144, 8192], P(('groups', 'req')), parts along dimension 0, may hold values from -6 to 6
- attn_mixed: bfloat16 [6144, 8192], P(('groups', 'req')), parts along dimension 0, may hold values from -6 to 6
- adapter_ids: int32 [6144], P(('groups', 'req')), parts along dimension 0, may hold values from 0 to 15, as said below
- send_slot: int32 [6144], P(('groups', 'req')), parts along dimension 0, may hold values from 0 to 383, as said below
- padded_row: int32 [6144], P(('groups', 'req')), parts along dimension 0, may hold values from 0 to 510, as said below
- fetch_list: int32 [32, 2], P('groups'), parts along dimension 0, may hold values from 0 to 15, as said below
- shrink_panels: bfloat16 [16, 256, 8192], P(None, None, 'req'), may hold values from -0.0625 to 0.0625
- expand_qo: bfloat16 [16, 128, 8192], P(None, None, 'req'), may hold values from -0.75 to 0.75
- expand_kv: bfloat16 [16, 128, 1024], P(None, None, 'req'), may hold values from -0.75 to 0.75
Outputs:
- delta_q: bfloat16 [6144, 8192], P(('groups', 'req')), parts along dimension 0
- delta_k: bfloat16 [6144, 1024], P(('groups', 'req')), parts along dimension 0
- delta_v: bfloat16 [6144, 1024], P(('groups', 'req')), parts along dimension 0
- delta_o: bfloat16 [6144, 8192], P(('groups', 'req')), parts along dimension 0
The draws below stay inside these ranges and needn't reach their ends.
There are 2 independent parts, one for each index of `groups`. The reference program is written for one: setup_inputs(seed, part) draws one part's arguments, and reference() takes and returns one part's arrays. A program takes and returns all parts, laid end to end along the dimension named above; an argument that names none is the same for every part. Nothing has to cross between parts.
Inputs may be any that keep to these rules, and one draw needn't show every extreme that they name: `adapter_ids`: within one owner the tokens of each block of 128 rows name one adapter. `send_slot`: slots of one device's tokens are distinct; at most 24 tokens of one device go to one owner, and some owner receives 24 tokens from every device. `padded_row`: rows of one owner's tokens are distinct. `fetch_list`: each owner's list holds 2 different adapters.
All inputs are finite; a program needn't handle non-finite values.
Results may differ from the reference program's by a relative error of at most 0.0051.
Values may be sent and summed in bfloat16 or wider, within the bound.
No kernel may reach another device: no remote copies, remote signals or barrier semaphores. Data moves between devices by JAX's collectives and lax.ppermute only.
A program may use at most 192 MiB of HBM per device.

```python
import jax
import jax.numpy as jnp
from jax import lax

D = 8192
KV = 1024
ADAPTER_RANK = 64
BLK = 128
TOK_DEV = 192
ADAPTERS = 16
TOKENS = 3072
SLOT = 24
CAP = 512
N_REQ = 16


def token_layout(key):
    owners = N_REQ
    share = TOK_DEV // N_REQ
    pairs = owners // 2
    keys = jax.random.split(key, 10)
    busiest = jax.random.randint(keys[0], (), 0, owners - 1)
    busiest = jnp.where(busiest == owners - 2, owners - 1, busiest)
    signs = jax.random.randint(keys[1], (owners, pairs), -1, 2)
    pair_index = jnp.arange(pairs)
    forced = jnp.where(busiest % 2 == 0, 1, -1)
    signs = jnp.where(pair_index[None, :] == busiest // 2, forced, signs)
    helper_source = jax.random.randint(keys[2], (), 0, owners)
    last_fix = (pair_index[None, :] == pairs - 1) & (jnp.arange(owners)[:, None] == helper_source) & (busiest // 2 != pairs - 1)
    signs = jnp.where(last_fix, -1, signs)
    counts = jnp.stack([share * (1 + signs), share * (1 - signs)], axis=2).reshape(owners, owners)
    ends = jnp.cumsum(counts, axis=1)
    items = jnp.arange(TOK_DEV)
    owner_of = jnp.sum((items[None, :, None] >= ends[:, None, :]).astype(jnp.int32), axis=2)
    start_of = jnp.take_along_axis(ends - counts, owner_of, axis=1)
    position = items[None, :] - start_of
    before = jnp.cumsum(counts, axis=0) - counts
    arrival = jnp.take_along_axis(before, owner_of, axis=1) + position
    received = jnp.sum(counts, axis=0)
    owner_index = jnp.arange(owners)
    first_adapter = jax.random.randint(keys[3], (owners,), 0, ADAPTERS)
    second_adapter = (first_adapter + jax.random.randint(keys[4], (owners,), 1, ADAPTERS)) % ADAPTERS
    first_adapter = jnp.where(owner_index == busiest, 0, first_adapter)
    second_adapter = jnp.where(owner_index == busiest, ADAPTERS - 1, second_adapter)
    split_at = jax.random.randint(keys[5], (owners,), 1, jnp.maximum(received, 2))
    split_at = jnp.where(owner_index == busiest, 1, split_at)
    own_split = split_at[owner_of]
    in_first = arrival < own_split
    second_start = (own_split + BLK - 1) // BLK * BLK
    rows_sorted = jnp.where(in_first, arrival, second_start + arrival - own_split)
    ids_sorted = jnp.where(in_first, first_adapter[owner_of], second_adapter[owner_of])
    slots_sorted = owner_of * SLOT + position
    shuffles = jax.vmap(lambda sub: jax.random.permutation(sub, TOK_DEV))(jax.random.split(keys[6], owners))
    inverse = jnp.argsort(shuffles, axis=1, stable=True)
    ids_out = jnp.take_along_axis(ids_sorted, inverse, axis=1).reshape(TOKENS).astype(jnp.int32)
    slots_out = jnp.take_along_axis(slots_sorted, inverse, axis=1).reshape(TOKENS).astype(jnp.int32)
    rows_out = jnp.take_along_axis(rows_sorted, inverse, axis=1).reshape(TOKENS).astype(jnp.int32)
    owner_scores = jnp.where((received >= 2) & (owner_index != busiest), jax.random.permutation(keys[7], owners) + 1, 0)
    forced_owner = jnp.argmax(owner_scores)
    dropped = ((jax.random.randint(keys[8], (owners,), 0, 4) == 0) | (owner_index == forced_owner)) & (owner_index != busiest)
    offset_draw = jax.random.randint(keys[9], (owners,), 1, ADAPTERS - 1)
    spare_adapter = (second_adapter + offset_draw) % ADAPTERS
    spare_adapter = jnp.where(spare_adapter == first_adapter, (spare_adapter + 1) % ADAPTERS, spare_adapter)
    listed_second = jnp.where(dropped, spare_adapter, second_adapter)
    lists_out = jnp.stack([first_adapter, listed_second], axis=1).astype(jnp.int32)
    return (ids_out, slots_out, rows_out, lists_out)


def draw_adapter_ids(key, part):
    return token_layout(key)[0]


def draw_send_slot(key, part):
    return token_layout(key)[1]


def draw_padded_row(key, part):
    return token_layout(key)[2]


def draw_fetch_list(key, part):
    return token_layout(key)[3]


def levels(stream_key, extent, cuts, low, high):
    factor_of = 1.0
    for dim, parts in cuts:
        heights = jax.random.uniform(jax.random.fold_in(jax.random.fold_in(stream_key, 6), dim), (parts,), jnp.float32, low / len(cuts), high / len(cuts))
        factor_of = factor_of * jnp.repeat(jnp.exp(heights), extent[dim] // parts).reshape((-1,) + (1,) * (len(extent) - 1 - dim))
    return factor_of


def normal_values(stream_key, dims, width, limit, cuts=(), kind=jnp.bfloat16):
    level = levels(stream_key, dims, cuts, -0.22, 0.18) if cuts else 1.0
    entries = jax.random.normal(stream_key, dims, jnp.float32) * width * level
    return jnp.minimum(jnp.maximum(entries, -limit), limit).astype(kind)


def setup_inputs(seed: int = 0, part: int = 0) -> dict:
    streams_of = jax.random.split(jax.random.key(seed), 10)
    part_splits = jax.random.split(jax.random.fold_in(streams_of[9], part), 10)
    return {
        "normed_hidden": normal_values(part_splits[0], (TOKENS, D), 1.0, 6.0, ((0, 16),)),
        "attn_mixed": normal_values(part_splits[1], (TOKENS, D), 1.0, 6.0, ((0, 16),)),
        "adapter_ids": draw_adapter_ids(jax.random.fold_in(jax.random.fold_in(streams_of[9], part), 71), part),
        "send_slot": draw_send_slot(jax.random.fold_in(jax.random.fold_in(streams_of[9], part), 71), part),
        "padded_row": draw_padded_row(jax.random.fold_in(jax.random.fold_in(streams_of[9], part), 71), part),
        "fetch_list": draw_fetch_list(jax.random.fold_in(jax.random.fold_in(streams_of[9], part), 71), part),
        "shrink_panels": normal_values(streams_of[6], (ADAPTERS, 4 * ADAPTER_RANK, D), D ** -0.5, 0.0625, ((2, 16),)),
        "expand_qo": normal_values(streams_of[7], (ADAPTERS, 2 * ADAPTER_RANK, D), ADAPTER_RANK ** -0.5, 0.75, ((2, 16),)),
        "expand_kv": normal_values(streams_of[8], (ADAPTERS, 2 * ADAPTER_RANK, KV), ADAPTER_RANK ** -0.5, 0.75, ((2, 16),)),
    }


adapter_scale_factor = 2.0


def reference(normed_hidden, attn_mixed, adapter_ids, send_slot, padded_row, fetch_list, shrink_panels, expand_qo, expand_kv):
    owner_of = send_slot // SLOT
    placed = (owner_of * CAP + padded_row).astype(jnp.int32)
    block_count = N_REQ * CAP // BLK
    block_of = placed // BLK
    block_adapter = jnp.full((block_count,), -1, jnp.int32).at[block_of].max(adapter_ids)
    block_owner = jnp.arange(block_count, dtype=jnp.int32) // (CAP // BLK)
    listed = jnp.any(fetch_list[block_owner] == block_adapter[:, None], axis=1) & (block_adapter >= 0)
    safe_adapter = jnp.maximum(block_adapter, 0)
    model_width = normed_hidden.shape[1]
    padded_x = jnp.zeros((N_REQ * CAP, model_width), jnp.bfloat16).at[placed].set(normed_hidden)
    padded_y = jnp.zeros((N_REQ * CAP, model_width), jnp.bfloat16).at[placed].set(attn_mixed)

    def one_block(pieces):
        block_x, block_y, adapter, keeper = pieces
        panel = shrink_panels[adapter]
        shrink_x = jnp.dot(block_x, panel[:3 * ADAPTER_RANK].T, preferred_element_type=jnp.float32)
        shrink_y = jnp.dot(block_y, panel[3 * ADAPTER_RANK:].T, preferred_element_type=jnp.float32)
        reduced_rows = (jnp.concatenate([shrink_x, shrink_y], axis=1) * keeper).astype(jnp.bfloat16)
        query_output_pair = expand_qo[adapter]
        key_value_pair = expand_kv[adapter]
        query_portion = (adapter_scale_factor * jnp.dot(reduced_rows[:, :ADAPTER_RANK], query_output_pair[:ADAPTER_RANK], preferred_element_type=jnp.float32)).astype(jnp.bfloat16)
        key_portion = (adapter_scale_factor * jnp.dot(reduced_rows[:, ADAPTER_RANK:2 * ADAPTER_RANK], key_value_pair[:ADAPTER_RANK], preferred_element_type=jnp.float32)).astype(jnp.bfloat16)
        value_portion = (adapter_scale_factor * jnp.dot(reduced_rows[:, 2 * ADAPTER_RANK:3 * ADAPTER_RANK], key_value_pair[ADAPTER_RANK:], preferred_element_type=jnp.float32)).astype(jnp.bfloat16)
        output_portion = (adapter_scale_factor * jnp.dot(reduced_rows[:, 3 * ADAPTER_RANK:], query_output_pair[ADAPTER_RANK:], preferred_element_type=jnp.float32)).astype(jnp.bfloat16)
        return query_portion, key_portion, value_portion, output_portion

    results = lax.map(one_block, (padded_x.reshape(block_count, BLK, model_width), padded_y.reshape(block_count, BLK, model_width), safe_adapter, listed.astype(jnp.float32)))
    whole_q = results[0].reshape(N_REQ * CAP, -1)
    whole_k = results[1].reshape(N_REQ * CAP, -1)
    whole_v = results[2].reshape(N_REQ * CAP, -1)
    whole_o = results[3].reshape(N_REQ * CAP, -1)
    return (whole_q[placed], whole_k[placed], whole_v[placed], whole_o[placed])
```

```python
import functools

import jax
import jax.numpy as jnp
from jax import lax
from jax.experimental import pallas as pl
from jax.experimental.pallas import tpu as pltpu
from jax.sharding import Mesh, PartitionSpec as P

LANES = 128
SET = 8
RANK = 64
SCALE = 2.0
VMEM_LIMIT = 48 * 1024 * 1024
PLANE = ("groups", "r")


def nt_dot(left, right):
    return lax.dot_general(
        left, right, (((1,), (1,)), ((), ())), preferred_element_type=jnp.float32
    )


def piece_offset(h, k, count, width):
    if count == 1:
        return 0
    start = lax.rem(h - k + count, count) * width
    return pl.multiple_of(start, LANES)


def shrink_kernel(ids_ref, tokens_ref, *rest):
    piece_refs, out_ref = rest[:-1], rest[-1]
    adapters, ranks, width = piece_refs[0].shape
    ids = ids_ref[...]
    pair_of = ids >> 1
    wide = jnp.zeros((tokens_ref.shape[0], 2 * ranks), jnp.float32)
    for first in range(0, adapters, 4):
        part = None
        for k, piece in enumerate(piece_refs):
            panel = piece[first : first + 4].reshape(4 * ranks, width)
            term = nt_dot(tokens_ref[:, k * width : (k + 1) * width], panel)
            part = term if part is None else part + term
        for j in range(2):
            wide = jnp.where(
                pair_of == first // 2 + j,
                part[:, 2 * j * ranks : 2 * (j + 1) * ranks],
                wide,
            )
    odd = (ids & 1) == 1
    out_ref[...] = jnp.where(odd, wide[:, ranks:], wide[:, :ranks]).astype(out_ref.dtype)


def shrink(ids, tokens, pieces, tile):
    rows, columns = tokens.shape
    adapters, ranks, width = pieces[0].shape
    return pl.pallas_call(
        shrink_kernel,
        grid=(rows // tile,),
        in_specs=[
            pl.BlockSpec((tile, 1), lambda i: (i, 0)),
            pl.BlockSpec((tile, columns), lambda i: (i, 0)),
        ]
        + [pl.BlockSpec((adapters, ranks, width), lambda i: (0, 0, 0))] * len(pieces),
        out_specs=pl.BlockSpec((tile, ranks), lambda i: (i, 0)),
        out_shape=jax.ShapeDtypeStruct((rows, ranks), jnp.bfloat16),
        compiler_params=pltpu.CompilerParams(vmem_limit_bytes=VMEM_LIMIT),
        cost_estimate=pl.CostEstimate(
            flops=2 * rows * columns * ranks * adapters,
            bytes_accessed=2 * (rows + adapters * ranks) * columns,
            transcendentals=0,
        ),
        name="shrink",
    )(ids, tokens, *pieces)


def expand_kernel(ids_ref, low_ref, *rest):
    piece_refs, out_ref = rest[:-1], rest[-1]
    adapters, ranks, width = piece_refs[0].shape
    ids = ids_ref[...]
    low = low_ref[...]
    spread = jnp.concatenate([low] * adapters, axis=1)
    lane_adapter = lax.broadcasted_iota(jnp.int32, spread.shape, 1) // ranks
    spread = jnp.where(lane_adapter == ids, spread, jnp.zeros_like(spread))
    for k, piece in enumerate(piece_refs):
        panel = piece[...].reshape(adapters * ranks, width)
        full = jnp.dot(spread, panel, preferred_element_type=jnp.float32)
        out_ref[:, k * width : (k + 1) * width] = (SCALE * full).astype(out_ref.dtype)


def expand(ids, low, pieces, tile):
    rows, ranks = low.shape
    adapters, _, width = pieces[0].shape
    columns = width * len(pieces)
    return pl.pallas_call(
        expand_kernel,
        grid=(rows // tile,),
        in_specs=[
            pl.BlockSpec((tile, 1), lambda i: (i, 0)),
            pl.BlockSpec((tile, ranks), lambda i: (i, 0)),
        ]
        + [pl.BlockSpec((adapters, ranks, width), lambda i: (0, 0, 0))] * len(pieces),
        out_specs=pl.BlockSpec((tile, columns), lambda i: (i, 0)),
        out_shape=jax.ShapeDtypeStruct((rows, columns), jnp.bfloat16),
        compiler_params=pltpu.CompilerParams(vmem_limit_bytes=VMEM_LIMIT),
        cost_estimate=pl.CostEstimate(
            flops=2 * rows * columns * ranks * adapters,
            bytes_accessed=2 * (rows + adapters * ranks) * columns,
            transcendentals=0,
        ),
        name="expand",
    )(ids, low, *pieces)


def exchange(array):
    return lax.all_to_all(array, PLANE, split_axis=0, concat_axis=0, tiled=True)


def ring(array, count):
    pieces = [array]
    order = [(k, (k + 1) % count) for k in range(count)]
    for _ in range(count - 1):
        pieces.append(lax.ppermute(pieces[-1], "h", order))
    return pieces


def in_lanes(pieces):
    if pieces[0].shape[2] % LANES == 0:
        return pieces
    return [jnp.concatenate(pieces, axis=2)]


def relative(h, count):
    return lax.rem(h - jnp.arange(count) + count, count)


def pack(array, h, count, inner, groups):
    rows, columns = array.shape
    width = columns // (count * inner * groups)
    cut = array.reshape(rows, count, inner, groups, width)
    cut = cut[:, relative(h, count)]
    return cut.transpose(3, 2, 0, 1, 4).reshape(groups * inner, rows, count * width)


def unpack(array, h, count, inner, groups):
    rows = array.shape[1]
    width = array.shape[2] // count
    cut = array.reshape(groups, inner, rows, count, width).transpose(2, 3, 1, 0, 4)
    cut = cut[:, relative(h, count)]
    return cut.reshape(rows, count * inner * groups * width)


def shards(
    normed_hidden,
    attn_mixed,
    adapter_ids,
    send_slot,
    padded_row,
    fetch_list,
    shrink_panels,
    expand_qo,
    expand_kv,
):
    groups, count, inner = (lax.axis_size(a) for a in ("groups", "h", "r"))
    g, h = lax.axis_index("groups"), lax.axis_index("h")
    devices = count * inner
    members = groups * inner
    tok_rows = normed_hidden.shape[0]
    slot_rows = 2 * tok_rows // devices
    rows = members * tok_rows
    tile = 2 * tok_rows

    listed = fetch_list[send_slot // slot_rows]
    keep = jnp.any(listed == adapter_ids[:, None], axis=1)
    own_ids = jnp.where(keep, adapter_ids, -1)
    ids = exchange(jnp.broadcast_to(own_ids, (members, tok_rows))).reshape(rows, 1)

    def own_columns(panel):
        width = panel.shape[2] // groups
        return lax.dynamic_slice_in_dim(panel, g * width, width, 2)

    panel_a = own_columns(shrink_panels)
    panel_b = own_columns(expand_qo)
    if groups == 2:
        panel_kv = lax.dynamic_slice_in_dim(expand_kv, g * RANK, RANK, 1)
    else:
        panel_kv = own_columns(expand_kv)
    a_o = in_lanes(ring(panel_a[:, 3 * RANK :], count))
    a_qkv = in_lanes(ring(panel_a[:, : 3 * RANK], count))
    b_kv = in_lanes(ring(panel_kv, count))
    b_q = in_lanes(ring(panel_b[:, :RANK], count))
    b_o = in_lanes(ring(panel_b[:, RANK:], count))

    def low_rows(tokens, pieces):
        sent = exchange(pack(tokens, h, count, inner, groups))
        part = shrink(ids, sent.reshape(rows, -1), pieces, tile)
        parts = exchange(part.reshape(members, tok_rows, -1))
        low = jnp.sum(parts.astype(jnp.float32), axis=0).astype(jnp.bfloat16)
        return lax.all_gather(low, PLANE, axis=0, tiled=True)

    def home(low, pieces):
        full = expand(ids, low, pieces, tile)
        return exchange(full.reshape(members, tok_rows, -1))

    low_o = low_rows(attn_mixed, a_o)
    low_qkv = low_rows(normed_hidden, a_qkv)
    low_k, low_v = low_qkv[:, RANK : 2 * RANK], low_qkv[:, 2 * RANK :]
    if groups == 2:
        both = home(jnp.where(g == 0, low_k, low_v), b_kv)
        half = both.reshape(2, inner, tok_rows, -1)
        delta_k = unpack(half[0], h, count, inner, 1)
        delta_v = unpack(half[1], h, count, inner, 1)
    else:
        panel = b_kv[0]
        delta_k = unpack(home(low_k, [panel[:, :RANK]]), h, count, inner, groups)
        delta_v = unpack(home(low_v, [panel[:, RANK:]]), h, count, inner, groups)
    delta_q = unpack(home(low_qkv[:, :RANK], b_q), h, count, inner, groups)
    delta_o = unpack(home(low_o, b_o), h, count, inner, groups)
    return delta_q, delta_k, delta_v, delta_o


def solution(mesh):
    groups, devices = mesh.devices.shape
    inner = max(SET // groups, 1)
    cut = Mesh(mesh.devices.reshape(groups, devices // inner, inner), ("groups", "h", "r"))
    by_token = P(("groups", "h", "r"))
    by_token_rows = P(("groups", "h", "r"), None)
    by_column = P(None, None, ("h", "r"))
    in_specs = (
        (by_token_rows,) * 2 + (by_token,) * 3 + (P("groups", None),) + (by_column,) * 3
    )
    out_specs = (by_token_rows,) * 4
    return jax.shard_map(shards, mesh=cut, in_specs=in_specs, out_specs=out_specs, check_vma=False)
```

```python
import functools

import jax
import jax.numpy as jnp
from jax import lax
from jax.experimental import pallas as pl
from jax.experimental.pallas import tpu as pltpu
from jax.sharding import Mesh, PartitionSpec as P

LANES = 128
CHUNK = 48
SET = 8
RANK = 64
SCALE = 2.0
VMEM_LIMIT = 48 * 1024 * 1024
PLANE = ("groups", "r")
REQ = ("h", "r")


def call(kernel, name, out_shape, flops, traffic, **kwargs):
    return pl.pallas_call(
        kernel,
        out_shape=out_shape,
        compiler_params=pltpu.CompilerParams(vmem_limit_bytes=VMEM_LIMIT),
        cost_estimate=pl.CostEstimate(flops=flops, bytes_accessed=traffic, transcendentals=0),
        name=name,
        **kwargs,
    )


def bf16(*shape):
    return jax.ShapeDtypeStruct(shape, jnp.bfloat16)


def nt_dot(left, right):
    return lax.dot_general(
        left, right, (((1,), (1,)), ((), ())), preferred_element_type=jnp.float32
    )


def shrink_rows(ids, tokens, panel_of, adapters, ranks):
    pair_of = ids >> 1
    wide = jnp.zeros((ids.shape[0], 2 * ranks), jnp.float32)
    for first in range(0, adapters, 4):
        part = None
        for tokens_piece, panel in zip(tokens, panel_of(first)):
            term = nt_dot(tokens_piece, panel.reshape(4 * ranks, panel.shape[2]))
            part = term if part is None else part + term
        for j in range(2):
            at = 2 * j * ranks
            wide = jnp.where(pair_of == first // 2 + j, part[:, at : at + 2 * ranks], wide)
    return jnp.where((ids & 1) == 1, wide[:, ranks:], wide[:, :ranks])


def shrink_kernel(ranks, ids_ref, tokens_ref, panel_ref, out_ref):
    low = shrink_rows(
        ids_ref[...],
        [tokens_ref[...]],
        lambda first: [panel_ref[first : first + 4, :ranks]],
        panel_ref.shape[0],
        ranks,
    )
    out_ref[...] = low.astype(out_ref.dtype).reshape(out_ref.shape)


def shrink(ids, tokens, panels, ranks, inner, tok_rows):
    rows, columns = tokens.shape
    adapters, held, _ = panels.shape
    tile = inner * tok_rows
    return call(
        functools.partial(shrink_kernel, ranks),
        "shrink",
        bf16(inner, rows // tile, tok_rows, ranks),
        2 * rows * columns * ranks * adapters,
        2 * (rows + adapters * held) * columns,
        grid=(rows // tile,),
        in_specs=[
            pl.BlockSpec((tile, 1), lambda i: (i, 0)),
            pl.BlockSpec((tile, columns), lambda i: (i, 0)),
            pl.BlockSpec((adapters, held, columns), lambda i: (0, 0, 0)),
        ],
        out_specs=pl.BlockSpec((inner, 1, tok_rows, ranks), lambda i: (0, i, 0, 0)),
    )(ids, tokens, panels)


def shrink_parts_kernel(ids_ref, panel_ref, *refs):
    pieces, adapters, ranks, width = panel_ref.shape
    members = len(refs) // 2
    rows = refs[0].shape[0]
    for s in range(0, members, 2):
        both = jnp.concatenate([refs[s][...], refs[s + 1][...]], axis=0)
        low = shrink_rows(
            ids_ref[s * rows : (s + 2) * rows],
            [both[:, k * width : (k + 1) * width] for k in range(pieces)],
            lambda first: [panel_ref[k, first : first + 4] for k in range(pieces)],
            adapters,
            ranks,
        ).astype(jnp.bfloat16)
        refs[members + s][...] = low[:rows]
        refs[members + s + 1][...] = low[rows:]


def shrink_parts(ids, tokens, panels):
    members, (rows, columns) = len(tokens), tokens[0].shape
    pieces, adapters, ranks, width = panels.shape
    vmem = pl.BlockSpec(memory_space=pltpu.VMEM)
    return call(
        shrink_parts_kernel,
        "shrink_parts",
        [bf16(rows, ranks)] * members,
        2 * members * rows * columns * ranks * adapters,
        2 * (members * rows + adapters * ranks) * columns,
        in_specs=[vmem] * (2 + members),
        out_specs=[vmem] * members,
    )(ids, panels, *tokens)


def spread_rows(ids, low, adapters):
    spread = jnp.concatenate([low] * adapters, axis=1)
    lane_adapter = lax.broadcasted_iota(jnp.int32, spread.shape, 1) // low.shape[1]
    return jnp.where(lane_adapter == ids, spread, jnp.zeros_like(spread))


def expand_kernel(ids_ref, low_ref, panel_ref, out_ref):
    pieces, adapters, _, width = panel_ref.shape
    ranks = low_ref.shape[1]
    spread = spread_rows(ids_ref[...], low_ref[...], adapters)
    for k in range(pieces):
        panel = panel_ref[k, :, :ranks].reshape(adapters * ranks, width)
        full = jnp.dot(spread, panel, preferred_element_type=jnp.float32)
        out_ref[:, k * width : (k + 1) * width] = (SCALE * full).astype(out_ref.dtype)


def expand(ids, low, panels, tile):
    rows, ranks = low.shape
    pieces, adapters, _, width = panels.shape
    columns = width * pieces
    return call(
        expand_kernel,
        "expand",
        bf16(rows, columns),
        2 * rows * columns * ranks * adapters,
        2 * (rows + adapters * ranks) * columns,
        grid=(rows // tile,),
        in_specs=[
            pl.BlockSpec((tile, 1), lambda i: (i, 0)),
            pl.BlockSpec((tile, ranks), lambda i: (i, 0)),
            pl.BlockSpec(panels.shape, lambda i: (0, 0, 0, 0)),
        ],
        out_specs=pl.BlockSpec((tile, columns), lambda i: (i, 0)),
    )(ids, low, panels)


def expand_joint_kernel(g_ref, ids_ref, low_ref, panel_ref, out_ref):
    pieces, adapters, folded, width = panel_ref.shape
    ranks = low_ref.shape[1] // 3
    rows = folded - ranks
    narrow = rows * width // ranks
    ids = ids_ref[...]
    spread = spread_rows(ids, low_ref[:, :ranks], adapters)
    for k in range(pieces):
        panel = panel_ref[k, :, :ranks].reshape(adapters * ranks, width)
        full = jnp.dot(spread, panel, preferred_element_type=jnp.float32)
        out_ref[:, k * width : (k + 1) * width] = (SCALE * full).astype(out_ref.dtype)
    low_kv = jnp.where(g_ref[0] == 0, low_ref[:, ranks : 2 * ranks], low_ref[:, 2 * ranks :])
    spread = spread_rows(ids, low_kv, adapters)
    wide = []
    for k in range(pieces):
        parts = [
            panel_ref[k, :, ranks:, j * narrow : (j + 1) * narrow]
            for j in range(ranks // rows)
        ]
        wide.append(jnp.concatenate(parts, axis=1))
    panel = jnp.concatenate(wide, axis=2).reshape(adapters * ranks, pieces * narrow)
    full = jnp.dot(spread, panel, preferred_element_type=jnp.float32)
    out_ref[:, pieces * width :] = (SCALE * full).astype(out_ref.dtype)


def expand_joint(g, ids, low, panels, tile):
    rows, ranks = low.shape[0], low.shape[1] // 3
    pieces, adapters, folded, width = panels.shape
    columns = pieces * (width + (folded - ranks) * width // ranks)
    return call(
        expand_joint_kernel,
        "expand_joint",
        bf16(rows, columns),
        2 * rows * columns * ranks * adapters,
        2 * (rows + adapters * ranks) * columns,
        grid=(rows // tile,),
        in_specs=[
            pl.BlockSpec(memory_space=pltpu.SMEM),
            pl.BlockSpec((tile, 1), lambda i: (i, 0)),
            pl.BlockSpec((tile, 3 * ranks), lambda i: (i, 0)),
            pl.BlockSpec(panels.shape, lambda i: (0, 0, 0, 0)),
        ],
        out_specs=pl.BlockSpec((tile, columns), lambda i: (i, 0)),
    )(g, ids, low, panels)


def expand_parts_kernel(p_ref, ids_ref, low_ref, panel_ref, *out_refs):
    pieces, adapters, ranks, width = panel_ref.shape
    rows = low_ref.shape[1]
    for s in range(0, len(out_refs), 2):
        pair = [low_ref[p_ref[0] ^ s], low_ref[p_ref[0] ^ (s + 1)]]
        spread = spread_rows(
            ids_ref[s * rows : (s + 2) * rows], jnp.concatenate(pair, axis=0), adapters
        )
        for k in range(pieces):
            panel = panel_ref[k].reshape(adapters * ranks, width)
            full = jnp.dot(spread, panel, preferred_element_type=jnp.float32)
            full = (SCALE * full).astype(jnp.bfloat16)
            out_refs[s][:, k * width : (k + 1) * width] = full[:rows]
            out_refs[s + 1][:, k * width : (k + 1) * width] = full[rows:]


def expand_parts(p, ids, low, panels):
    members, rows, ranks = low.shape
    pieces, adapters, _, width = panels.shape
    columns = pieces * width
    vmem = pl.BlockSpec(memory_space=pltpu.VMEM)
    return call(
        expand_parts_kernel,
        "expand_parts",
        [bf16(rows, columns)] * members,
        2 * members * rows * columns * ranks * adapters,
        2 * (members * rows + adapters * ranks) * columns,
        in_specs=[pl.BlockSpec(memory_space=pltpu.SMEM)] + [vmem] * 3,
        out_specs=[vmem] * members,
    )(p, ids, low, panels)


def exchange(array, axes):
    return lax.all_to_all(array, axes, split_axis=0, concat_axis=0, tiled=True)


def swap_parts(parts):
    members = len(parts)
    return [parts[0]] + [
        lax.ppermute(parts[s], PLANE, [(d, d ^ s) for d in range(members)])
        for s in range(1, members)
    ]


def along_h(array):
    pieces = lax.all_gather(array, "h", axis=0)
    if array.shape[2] % LANES == 0:
        return pieces
    return pieces.transpose(1, 2, 0, 3).reshape((1,) + array.shape[:2] + (-1,))


def piece_places(member, count, inner, groups):
    g, r = member // inner, member % inner
    return [(k * inner + r) * groups + g for k in range(count)]


def window(place, width):
    start = place * width
    return pl.ds(start if isinstance(start, int) else pl.multiple_of(start, width), width)


def pack_parts_kernel(count, inner, groups, p_ref, source_ref, *out_refs):
    width = out_refs[0].shape[1] // count
    for s, out_ref in enumerate(out_refs):
        places = piece_places(p_ref[0] ^ s, count, inner, groups)
        for k, place in enumerate(places):
            out_ref[:, k * width : (k + 1) * width] = source_ref[:, window(place, width)]


def pack_parts(array, p, count, inner, groups):
    rows, columns = array.shape
    members = groups * inner
    width = columns // (count * members)
    if width % LANES:
        cut = array.reshape(rows, count, inner, groups, width).transpose(3, 2, 0, 1, 4)
        cut = cut.reshape(members, rows, count * width)
        return [lax.dynamic_index_in_dim(cut, p[0] ^ s, keepdims=False) for s in range(members)]
    return call(
        functools.partial(pack_parts_kernel, count, inner, groups),
        "pack_parts",
        [bf16(rows, count * width)] * members,
        0,
        4 * rows * columns,
        grid_spec=pltpu.PrefetchScalarGridSpec(
            num_scalar_prefetch=1,
            grid=(rows // CHUNK,),
            in_specs=[pl.BlockSpec((CHUNK, columns), lambda i, p_ref: (i, 0))],
            out_specs=[pl.BlockSpec((CHUNK, count * width), lambda i, p_ref: (i, 0))] * members,
        ),
    )(p, array)


def unpack_parts_kernel(count, inner, groups, p_ref, *refs):
    out_ref = refs[-1]
    width = refs[0].shape[1] // count
    for s, part_ref in enumerate(refs[:-1]):
        places = piece_places(p_ref[0] ^ s, count, inner, groups)
        for k, place in enumerate(places):
            out_ref[:, window(place, width)] = part_ref[:, k * width : (k + 1) * width]


def unpack_parts(parts, p, count, inner, groups):
    members, (rows, columns) = len(parts), parts[0].shape
    if (columns // count) % LANES:
        stacked = jnp.stack(parts)[p[0] ^ jnp.arange(members)]
        return unpack(stacked, count, inner, groups)
    return call(
        functools.partial(unpack_parts_kernel, count, inner, groups),
        "unpack_parts",
        bf16(rows, columns * members),
        0,
        4 * rows * columns * members,
        grid_spec=pltpu.PrefetchScalarGridSpec(
            num_scalar_prefetch=1,
            grid=(rows // CHUNK,),
            in_specs=[pl.BlockSpec((CHUNK, columns), lambda i, p_ref: (i, 0))] * members,
            out_specs=pl.BlockSpec((CHUNK, columns * members), lambda i, p_ref: (i, 0)),
        ),
    )(p, *parts)


def unpack_kernel(count, inner, groups, source_ref, out_ref):
    members, _, columns = source_ref.shape
    width = columns // count
    for m in range(members):
        for k, place in enumerate(piece_places(m, count, inner, groups)):
            out_ref[:, window(place, width)] = source_ref[m, :, k * width : (k + 1) * width]


def unpack(array, count, inner, groups):
    members, rows, columns = array.shape
    width = columns // count
    shape = (rows, columns * members)
    if width % LANES:
        cut = array.reshape(groups, inner, rows, count, width).transpose(2, 3, 1, 0, 4)
        return cut.reshape(shape)
    return call(
        functools.partial(unpack_kernel, count, inner, groups),
        "unpack",
        bf16(*shape),
        0,
        4 * array.size,
        grid=(rows // CHUNK,),
        in_specs=[pl.BlockSpec((members, CHUNK, columns), lambda i: (0, i, 0))],
        out_specs=pl.BlockSpec((CHUNK, columns * members), lambda i: (i, 0)),
    )(array)


def pack_kernel(source_ref, out_ref):
    width = out_ref.shape[2]
    for m in range(out_ref.shape[0]):
        out_ref[m] = source_ref[:, m * width : (m + 1) * width]


def pack(array, members):
    rows, columns = array.shape
    width = columns // members
    return call(
        pack_kernel,
        "pack",
        bf16(members, rows, width),
        0,
        4 * array.size,
        grid=(rows // CHUNK,),
        in_specs=[pl.BlockSpec((CHUNK, columns), lambda i: (i, 0))],
        out_specs=pl.BlockSpec((members, CHUNK, width), lambda i: (0, i, 0)),
    )(array)


def unpack_joint_kernel(count, inner, groups, narrow, parts_ref, q_ref, k_ref, v_ref):
    members, _, columns = parts_ref.shape
    width = columns // count - narrow
    for m in range(members):
        for k, place in enumerate(piece_places(m, count, inner, groups)):
            q_ref[:, window(place, width)] = parts_ref[m, :, k * width : (k + 1) * width]
    for start, out_ref in ((0, k_ref), (inner, v_ref)):
        for h in range(count):
            for r in range(0, inner, 2):
                at = count * width + h * narrow
                pair = [parts_ref[start + r + j, :, at : at + narrow] for j in range(2)]
                at = (h * inner + r) * narrow
                out_ref[:, at : at + 2 * narrow] = jnp.concatenate(pair, axis=1)


def unpack_joint(parts, narrow, count, inner, groups):
    members, rows, columns = parts.shape
    q_columns = (columns - count * narrow) * members
    kv_columns = count * inner * narrow
    return call(
        functools.partial(unpack_joint_kernel, count, inner, groups, narrow),
        "unpack_joint",
        (bf16(rows, q_columns), bf16(rows, kv_columns), bf16(rows, kv_columns)),
        0,
        4 * parts.size,
        grid=(rows // CHUNK,),
        in_specs=[pl.BlockSpec((members, CHUNK, columns), lambda i: (0, i, 0))],
        out_specs=[
            pl.BlockSpec((CHUNK, q_columns), lambda i: (i, 0)),
            pl.BlockSpec((CHUNK, kv_columns), lambda i: (i, 0)),
            pl.BlockSpec((CHUNK, kv_columns), lambda i: (i, 0)),
        ],
    )(parts)


def shards(
    normed_hidden,
    attn_mixed,
    adapter_ids,
    send_slot,
    padded_row,
    fetch_list,
    shrink_panels,
    expand_qo,
    expand_kv,
):
    groups, count, inner = (lax.axis_size(a) for a in ("groups", "h", "r"))
    g, h, r = (lax.axis_index(a) for a in ("groups", "h", "r"))
    p = (g * inner + r).reshape(1)
    devices = count * inner
    members = groups * inner
    tok_rows = normed_hidden.shape[0]
    slot_rows = 2 * tok_rows // devices
    rows = members * tok_rows
    tile = 2 * tok_rows

    def own_columns(panel):
        width = panel.shape[2] // groups
        return lax.dynamic_slice_in_dim(panel, g * width, width, 2)

    own_q = own_columns(expand_qo[:, :RANK])
    fold = groups == 2 and own_q.shape[2] % LANES == 0
    if fold:
        own_kv = lax.dynamic_slice_in_dim(expand_kv, g * RANK, RANK, 1)
        folds = own_q.shape[2] // own_kv.shape[2]
        own_kv = jnp.concatenate(jnp.split(own_kv, folds, axis=1), axis=2)
        b_q = along_h(jnp.concatenate([own_q, own_kv], axis=1))
    else:
        b_q = along_h(own_q)
        b_kv = along_h(own_columns(expand_kv))

    a_o = along_h(own_columns(shrink_panels[:, 3 * RANK :]))

    listed = fetch_list[send_slot // slot_rows]
    keep = jnp.any(listed == adapter_ids[:, None], axis=1)
    own_ids = jnp.where(keep, adapter_ids, -1)
    group_ids = exchange(jnp.broadcast_to(own_ids, (devices, tok_rows)), REQ)
    near_ids = lax.dynamic_slice_in_dim(group_ids, h * inner, inner, 0)
    if groups == 2:
        far_ids = lax.ppermute(near_ids, "groups", [(0, 1), (1, 0)])
        first, second = jnp.where(g == 0, near_ids, far_ids), jnp.where(g == 0, far_ids, near_ids)
        plane_ids = jnp.concatenate([first, second], axis=0)
    else:
        plane_ids = lax.all_gather(near_ids, "groups", axis=0, tiled=True)
    swap_ids = plane_ids[p ^ jnp.arange(members)].reshape(rows, 1)
    plane_ids = plane_ids.reshape(rows, 1)
    group_ids = group_ids.reshape(devices * tok_rows, 1)

    packed_x = pack(normed_hidden, devices)
    sent_x = exchange(packed_x, REQ)
    attn_mixed, packed_x = lax.optimization_barrier((attn_mixed, packed_x))
    sent_y = swap_parts(pack_parts(attn_mixed, p, count, inner, groups))

    sent_x, sent_y, group_ids, swap_ids, plane_ids = lax.optimization_barrier(
        (sent_x, sent_y, group_ids, swap_ids, plane_ids)
    )
    tokens = sent_x.reshape(devices * tok_rows, -1)
    part = shrink(group_ids, tokens, shrink_panels, 3 * RANK, inner, tok_rows)
    part, a_o = lax.optimization_barrier((part, a_o))
    near = jnp.sum(exchange(part, "r").astype(jnp.float32), axis=0).astype(jnp.bfloat16)

    parts_o = swap_parts(shrink_parts(swap_ids, sent_y, a_o))
    low_o = sum(piece.astype(jnp.float32) for piece in parts_o).astype(jnp.bfloat16)
    near, low_o = lax.optimization_barrier((near, low_o))
    low_o = lax.all_gather(low_o, PLANE, axis=0)

    far = exchange(near, "h")
    far, low_o, own_o = lax.optimization_barrier((far, low_o, own_columns(expand_qo[:, RANK:])))
    b_o = along_h(own_o)
    low = jnp.sum(far.astype(jnp.float32), axis=0).astype(jnp.bfloat16)
    low = lax.all_gather(low, PLANE, axis=0, tiled=True)

    def home(low_part, panels):
        full = expand(plane_ids, low_part, panels, tile)
        return exchange(full.reshape(members, tok_rows, -1), PLANE)

    if fold:
        full = expand_joint(g.reshape(1), plane_ids, low, b_q, tile)
        full, low_o = lax.optimization_barrier((full, low_o))
        parts = exchange(full.reshape(members, tok_rows, -1), PLANE)
        narrow = expand_kv.shape[2]
        delta_q, delta_k, delta_v = unpack_joint(parts, narrow, count, inner, groups)
        full_o = expand_parts(p, swap_ids, low_o, b_o)
        delta_o = unpack_parts(swap_parts(full_o), p, count, inner, groups)
        return delta_q, delta_k, delta_v, delta_o
    full_o = expand_parts(p, swap_ids, low_o, b_o)
    delta_o = unpack_parts(swap_parts(full_o), p, count, inner, groups)
    low_k, low_v = low[:, RANK : 2 * RANK], low[:, 2 * RANK :]
    delta_k = unpack(home(low_k, b_kv[:, :, :RANK]), count, inner, groups)
    delta_v = unpack(home(low_v, b_kv[:, :, RANK:]), count, inner, groups)
    delta_q = unpack(home(low[:, :RANK], b_q), count, inner, groups)
    return delta_q, delta_k, delta_v, delta_o


def solution(mesh):
    groups, devices = mesh.devices.shape
    inner = max(SET // groups, 1)
    cut = Mesh(mesh.devices.reshape(groups, devices // inner, inner), ("groups", "h", "r"))
    by_token = P(("groups", "h", "r"))
    by_token_rows = P(("groups", "h", "r"), None)
    by_column = P(None, None, ("h", "r"))
    in_specs = (
        (by_token_rows,) * 2 + (by_token,) * 3 + (P("groups", None),) + (by_column,) * 3
    )
    out_specs = (by_token_rows,) * 4
    return jax.shard_map(shards, mesh=cut, in_specs=in_specs, out_specs=out_specs, check_vma=False)
```

```python
import functools

import jax
import jax.numpy as jnp
from jax import lax
from jax.experimental import pallas as pl
from jax.experimental.pallas import tpu as pltpu
from jax.sharding import Mesh, PartitionSpec as P

LANES = 128
CHUNK = 48
NOTE_ROWS = 16
SET = 8
RANK = 64
SCALE = 2.0
VMEM_LIMIT = 48 * 1024 * 1024
PLANE = ("groups", "r")
REQ = ("h", "r")


def call(kernel, name, out_shape, flops, traffic, **kwargs):
    return pl.pallas_call(
        kernel,
        out_shape=out_shape,
        compiler_params=pltpu.CompilerParams(vmem_limit_bytes=VMEM_LIMIT),
        cost_estimate=pl.CostEstimate(flops=flops, bytes_accessed=traffic, transcendentals=0),
        name=name,
        **kwargs,
    )


def bf16(*shape):
    return jax.ShapeDtypeStruct(shape, jnp.bfloat16)


def nt_dot(left, right):
    return lax.dot_general(
        left, right, (((1,), (1,)), ((), ())), preferred_element_type=jnp.float32
    )


def shrink_rows(ids, tokens, panel_of, adapters, ranks):
    pair_of = ids >> 1
    wide = jnp.zeros((ids.shape[0], 2 * ranks), jnp.float32)
    for first in range(0, adapters, 4):
        part = None
        for tokens_piece, panel in zip(tokens, panel_of(first)):
            term = nt_dot(tokens_piece, panel.reshape(4 * ranks, panel.shape[2]))
            part = term if part is None else part + term
        for j in range(2):
            at = 2 * j * ranks
            wide = jnp.where(pair_of == first // 2 + j, part[:, at : at + 2 * ranks], wide)
    return jnp.where((ids & 1) == 1, wide[:, ranks:], wide[:, :ranks])


def shrink_kernel(ranks, ids_ref, tokens_ref, panel_ref, out_ref):
    sources, rows = out_ref.shape[0], out_ref.shape[2]
    tokens = tokens_ref[:, :rows, :].reshape(sources * rows, tokens_ref.shape[2])
    low = shrink_rows(
        ids_ref[...],
        [tokens],
        lambda first: [panel_ref[first : first + 4, :ranks]],
        panel_ref.shape[0],
        ranks,
    )
    out_ref[...] = low.astype(out_ref.dtype).reshape(out_ref.shape)


def shrink(ids, tokens, panels, ranks, inner, tok_rows):
    sources, held_rows, columns = tokens.shape
    adapters, held, _ = panels.shape
    tile = inner * tok_rows
    steps = sources // inner
    return call(
        functools.partial(shrink_kernel, ranks),
        "shrink",
        bf16(inner, steps, tok_rows, ranks),
        2 * steps * tile * columns * ranks * adapters,
        2 * (steps * tile + adapters * held) * columns,
        grid=(steps,),
        in_specs=[
            pl.BlockSpec((tile, 1), lambda i: (i, 0)),
            pl.BlockSpec((inner, held_rows, columns), lambda i: (i, 0, 0)),
            pl.BlockSpec((adapters, held, columns), lambda i: (0, 0, 0)),
        ],
        out_specs=pl.BlockSpec((inner, 1, tok_rows, ranks), lambda i: (0, i, 0, 0)),
    )(ids, tokens, panels)


def shrink_parts_kernel(ids_ref, panel_ref, *refs):
    pieces, adapters, _, width = panel_ref.shape
    ranks = refs[-1].shape[1]
    members = len(refs) // 2
    rows = refs[0].shape[0]
    for s in range(0, members, 2):
        both = jnp.concatenate([refs[s][...], refs[s + 1][...]], axis=0)
        low = shrink_rows(
            ids_ref[s * rows : (s + 2) * rows],
            [both[:, k * width : (k + 1) * width] for k in range(pieces)],
            lambda first: [panel_ref[k, first : first + 4, :ranks] for k in range(pieces)],
            adapters,
            ranks,
        ).astype(jnp.bfloat16)
        refs[members + s][...] = low[:rows]
        refs[members + s + 1][...] = low[rows:]


def shrink_parts(ids, tokens, panels, ranks):
    members, (rows, columns) = len(tokens), tokens[0].shape
    adapters = panels.shape[1]
    vmem = pl.BlockSpec(memory_space=pltpu.VMEM)
    return call(
        shrink_parts_kernel,
        "shrink_parts",
        [bf16(rows, ranks)] * members,
        2 * members * rows * columns * ranks * adapters,
        2 * (members * rows + adapters * ranks) * columns,
        in_specs=[vmem] * (2 + members),
        out_specs=[vmem] * members,
    )(ids, panels, *tokens)


def spread_rows(ids, low, adapters):
    spread = jnp.concatenate([low] * adapters, axis=1)
    lane_adapter = lax.broadcasted_iota(jnp.int32, spread.shape, 1) // low.shape[1]
    return jnp.where(lane_adapter == ids, spread, jnp.zeros_like(spread))


def expand_kernel(ids_ref, low_ref, panel_ref, out_ref):
    pieces, adapters, _, width = panel_ref.shape
    ranks = low_ref.shape[1]
    spread = spread_rows(ids_ref[...], low_ref[...], adapters)
    for k in range(pieces):
        panel = panel_ref[k, :, :ranks].reshape(adapters * ranks, width)
        full = jnp.dot(spread, panel, preferred_element_type=jnp.float32)
        out_ref[:, k * width : (k + 1) * width] = (SCALE * full).astype(out_ref.dtype)


def expand(ids, low, panels, tile):
    rows, ranks = low.shape
    pieces, adapters, _, width = panels.shape
    columns = width * pieces
    return call(
        expand_kernel,
        "expand",
        bf16(rows, columns),
        2 * rows * columns * ranks * adapters,
        2 * (rows + adapters * ranks) * columns,
        grid=(rows // tile,),
        in_specs=[
            pl.BlockSpec((tile, 1), lambda i: (i, 0)),
            pl.BlockSpec((tile, ranks), lambda i: (i, 0)),
            pl.BlockSpec(panels.shape, lambda i: (0, 0, 0, 0)),
        ],
        out_specs=pl.BlockSpec((tile, columns), lambda i: (i, 0)),
    )(ids, low, panels)


def expand_joint_kernel(start, g_ref, ids_ref, low_ref, panel_ref, out_ref):
    pieces, adapters, held, width = panel_ref.shape
    ranks = low_ref.shape[1] // 4
    stop = start + ranks
    rows = held - stop
    narrow = rows * width // ranks
    ids = ids_ref[...]
    spread = spread_rows(ids, low_ref[:, :ranks], adapters)
    for k in range(pieces):
        panel = panel_ref[k, :, start:stop].reshape(adapters * ranks, width)
        full = jnp.dot(spread, panel, preferred_element_type=jnp.float32)
        out_ref[:, k * width : (k + 1) * width] = (SCALE * full).astype(out_ref.dtype)
    low_kv = [low_ref[:, j * ranks : (j + 1) * ranks] for j in (1, 2)]
    low_kv = jnp.where(g_ref[0] == 0, *low_kv)
    spread = spread_rows(ids, low_kv, adapters)
    wide = []
    for k in range(pieces):
        parts = [
            panel_ref[k, :, stop:, j * narrow : (j + 1) * narrow]
            for j in range(ranks // rows)
        ]
        wide.append(jnp.concatenate(parts, axis=1))
    panel = jnp.concatenate(wide, axis=2).reshape(adapters * ranks, pieces * narrow)
    full = jnp.dot(spread, panel, preferred_element_type=jnp.float32)
    out_ref[:, pieces * width :] = (SCALE * full).astype(out_ref.dtype)


def expand_joint(g, ids, low, panels, start, tile):
    rows, ranks = low.shape[0], low.shape[1] // 4
    pieces, adapters, held, width = panels.shape
    columns = pieces * (width + (held - start - ranks) * width // ranks)
    return call(
        functools.partial(expand_joint_kernel, start),
        "expand_joint",
        bf16(rows, columns),
        2 * rows * columns * ranks * adapters,
        2 * (rows + adapters * ranks) * columns,
        grid=(rows // tile,),
        in_specs=[
            pl.BlockSpec(memory_space=pltpu.SMEM),
            pl.BlockSpec((tile, 1), lambda i: (i, 0)),
            pl.BlockSpec((tile, 4 * ranks), lambda i: (i, 0)),
            pl.BlockSpec(panels.shape, lambda i: (0, 0, 0, 0)),
        ],
        out_specs=pl.BlockSpec((tile, columns), lambda i: (i, 0)),
    )(g, ids, low, panels)


def expand_parts_kernel(p_ref, ids_ref, low_ref, panel_ref, *out_refs):
    pieces, adapters, ranks, width = panel_ref.shape
    rows, start = low_ref.shape[1], low_ref.shape[2] - ranks
    for s in range(0, len(out_refs), 2):
        pair = [low_ref[p_ref[0] ^ (s + j), :, start:] for j in range(2)]
        spread = spread_rows(
            ids_ref[s * rows : (s + 2) * rows], jnp.concatenate(pair, axis=0), adapters
        )
        for k in range(pieces):
            panel = panel_ref[k].reshape(adapters * ranks, width)
            full = jnp.dot(spread, panel, preferred_element_type=jnp.float32)
            full = (SCALE * full).astype(jnp.bfloat16)
            out_refs[s][:, k * width : (k + 1) * width] = full[:rows]
            out_refs[s + 1][:, k * width : (k + 1) * width] = full[rows:]


def expand_parts(p, ids, low, panels):
    members, rows, _ = low.shape
    pieces, adapters, ranks, width = panels.shape
    columns = pieces * width
    vmem = pl.BlockSpec(memory_space=pltpu.VMEM)
    return call(
        expand_parts_kernel,
        "expand_parts",
        [bf16(rows, columns)] * members,
        2 * members * rows * columns * ranks * adapters,
        2 * (members * rows + adapters * ranks) * columns,
        in_specs=[pl.BlockSpec(memory_space=pltpu.SMEM)] + [vmem] * 3,
        out_specs=[vmem] * members,
    )(p, ids, low, panels)


def exchange(array, axes):
    return lax.all_to_all(array, axes, split_axis=0, concat_axis=0, tiled=True)


def swap_parts(parts):
    members = len(parts)
    return [parts[0]] + [
        lax.ppermute(parts[s], PLANE, [(d, d ^ s) for d in range(members)])
        for s in range(1, members)
    ]


def along_h(array):
    pieces = lax.all_gather(array, "h", axis=0)
    if array.shape[2] % LANES == 0:
        return pieces
    return pieces.transpose(1, 2, 0, 3).reshape((1,) + array.shape[:2] + (-1,))


def piece_places(member, count, inner, groups):
    g, r = member // inner, member % inner
    return [(k * inner + r) * groups + g for k in range(count)]


def window(place, width):
    start = place * width
    return pl.ds(start if isinstance(start, int) else pl.multiple_of(start, width), width)


def pack_parts_kernel(count, inner, groups, p_ref, source_ref, *out_refs):
    width = out_refs[0].shape[1] // count
    for s, out_ref in enumerate(out_refs):
        places = piece_places(p_ref[0] ^ s, count, inner, groups)
        for k, place in enumerate(places):
            out_ref[:, k * width : (k + 1) * width] = source_ref[:, window(place, width)]


def pack_parts(array, p, count, inner, groups):
    rows, columns = array.shape
    members = groups * inner
    width = columns // (count * members)
    if width % LANES:
        cut = array.reshape(rows, count, inner, groups, width).transpose(3, 2, 0, 1, 4)
        cut = cut.reshape(members, rows, count * width)
        return [lax.dynamic_index_in_dim(cut, p[0] ^ s, keepdims=False) for s in range(members)]
    return call(
        functools.partial(pack_parts_kernel, count, inner, groups),
        "pack_parts",
        [bf16(rows, count * width)] * members,
        0,
        4 * rows * columns,
        grid_spec=pltpu.PrefetchScalarGridSpec(
            num_scalar_prefetch=1,
            grid=(rows // CHUNK,),
            in_specs=[pl.BlockSpec((CHUNK, columns), lambda i, p_ref: (i, 0))],
            out_specs=[pl.BlockSpec((CHUNK, count * width), lambda i, p_ref: (i, 0))] * members,
        ),
    )(p, array)


def unpack_parts_kernel(count, inner, groups, p_ref, *refs):
    out_ref = refs[-1]
    width = refs[0].shape[1] // count
    for s, part_ref in enumerate(refs[:-1]):
        places = piece_places(p_ref[0] ^ s, count, inner, groups)
        for k, place in enumerate(places):
            out_ref[:, window(place, width)] = part_ref[:, k * width : (k + 1) * width]


def unpack_parts(parts, p, count, inner, groups):
    members, (rows, columns) = len(parts), parts[0].shape
    if (columns // count) % LANES:
        stacked = jnp.stack(parts)[p[0] ^ jnp.arange(members)]
        return unpack(stacked, count, inner, groups)
    return call(
        functools.partial(unpack_parts_kernel, count, inner, groups),
        "unpack_parts",
        bf16(rows, columns * members),
        0,
        4 * rows * columns * members,
        grid_spec=pltpu.PrefetchScalarGridSpec(
            num_scalar_prefetch=1,
            grid=(rows // CHUNK,),
            in_specs=[pl.BlockSpec((CHUNK, columns), lambda i, p_ref: (i, 0))] * members,
            out_specs=pl.BlockSpec((CHUNK, columns * members), lambda i, p_ref: (i, 0)),
        ),
    )(p, *parts)


def unpack_kernel(count, inner, groups, source_ref, out_ref):
    members, _, columns = source_ref.shape
    width = columns // count
    for m in range(members):
        for k, place in enumerate(piece_places(m, count, inner, groups)):
            out_ref[:, window(place, width)] = source_ref[m, :, k * width : (k + 1) * width]


def unpack(array, count, inner, groups):
    members, rows, columns = array.shape
    width = columns // count
    shape = (rows, columns * members)
    if width % LANES:
        cut = array.reshape(groups, inner, rows, count, width).transpose(2, 3, 1, 0, 4)
        return cut.reshape(shape)
    return call(
        functools.partial(unpack_kernel, count, inner, groups),
        "unpack",
        bf16(*shape),
        0,
        4 * array.size,
        grid=(rows // CHUNK,),
        in_specs=[pl.BlockSpec((members, CHUNK, columns), lambda i: (0, i, 0))],
        out_specs=pl.BlockSpec((CHUNK, columns * members), lambda i: (i, 0)),
    )(array)


def pack_kernel(steps, notes_ref, source_ref, out_ref):
    members, _, width = out_ref.shape

    @pl.when(pl.program_id(0) < steps)
    def _():
        for m in range(members):
            out_ref[m] = source_ref[:, m * width : (m + 1) * width]

    @pl.when(pl.program_id(0) == steps)
    def _():
        for m in range(members):
            out_ref[m] = notes_ref[...]


def pack(array, notes, members):
    rows, columns = array.shape
    chunk, width = notes.shape
    steps = rows // chunk
    return call(
        functools.partial(pack_kernel, steps),
        "pack",
        bf16(members, rows + chunk, width),
        0,
        4 * array.size,
        grid=(steps + 1,),
        in_specs=[
            pl.BlockSpec((chunk, width), lambda i: (0, 0)),
            pl.BlockSpec((chunk, columns), lambda i: (jnp.minimum(i, steps - 1), 0)),
        ],
        out_specs=pl.BlockSpec((members, chunk, width), lambda i: (0, i, 0)),
    )(notes, array)


def unpack_joint_kernel(count, inner, groups, narrow, parts_ref, q_ref, k_ref, v_ref):
    members, _, columns = parts_ref.shape
    width = columns // count - narrow
    for m in range(members):
        for k, place in enumerate(piece_places(m, count, inner, groups)):
            q_ref[:, window(place, width)] = parts_ref[m, :, k * width : (k + 1) * width]
    for start, out_ref in ((0, k_ref), (inner, v_ref)):
        for h in range(count):
            for r in range(0, inner, 2):
                at = count * width + h * narrow
                pair = [parts_ref[start + r + j, :, at : at + narrow] for j in range(2)]
                at = (h * inner + r) * narrow
                out_ref[:, at : at + 2 * narrow] = jnp.concatenate(pair, axis=1)


def unpack_joint(parts, narrow, count, inner, groups):
    members, rows, columns = parts.shape
    q_columns = (columns - count * narrow) * members
    kv_columns = count * inner * narrow
    return call(
        functools.partial(unpack_joint_kernel, count, inner, groups, narrow),
        "unpack_joint",
        (bf16(rows, q_columns), bf16(rows, kv_columns), bf16(rows, kv_columns)),
        0,
        4 * parts.size,
        grid=(rows // CHUNK,),
        in_specs=[pl.BlockSpec((members, CHUNK, columns), lambda i: (0, i, 0))],
        out_specs=[
            pl.BlockSpec((CHUNK, q_columns), lambda i: (i, 0)),
            pl.BlockSpec((CHUNK, kv_columns), lambda i: (i, 0)),
            pl.BlockSpec((CHUNK, kv_columns), lambda i: (i, 0)),
        ],
    )(parts)


def shards(
    normed_hidden,
    attn_mixed,
    adapter_ids,
    send_slot,
    padded_row,
    fetch_list,
    shrink_panels,
    expand_qo,
    expand_kv,
):
    groups, count, inner = (lax.axis_size(a) for a in ("groups", "h", "r"))
    g, h, r = (lax.axis_index(a) for a in ("groups", "h", "r"))
    p = (g * inner + r).reshape(1)
    devices = count * inner
    members = groups * inner
    tok_rows = normed_hidden.shape[0]
    slot_rows = 2 * tok_rows // devices
    rows = members * tok_rows
    tile = 2 * tok_rows

    def own_columns(panel):
        width = panel.shape[2] // groups
        return lax.dynamic_slice_in_dim(panel, g * width, width, 2)

    def finish_o(low_o, b_o):
        full_o = expand_parts(p, swap_ids, low_o, b_o)
        return unpack_parts(swap_parts(full_o), p, count, inner, groups)

    owner = send_slot // slot_rows
    at_owner = owner[:, None] == jnp.arange(devices)[None, :]
    listed = jnp.any(fetch_list[None] == adapter_ids[:, None, None], axis=2)
    own_ids = jnp.where(jnp.any(at_owner & listed, axis=1), adapter_ids, -1)
    notes = jnp.broadcast_to(own_ids.astype(jnp.bfloat16), (NOTE_ROWS, tok_rows))
    notes = jnp.pad(notes, ((0, 0), (0, normed_hidden.shape[1] // devices - tok_rows)))
    packed_x = pack(normed_hidden, notes, devices)
    sent_x = exchange(packed_x, REQ)

    attn_mixed, packed_x = lax.optimization_barrier((attn_mixed, packed_x))
    sent_y = swap_parts(pack_parts(attn_mixed, p, count, inner, groups))
    a_o = along_h(own_columns(shrink_panels[:, 3 * RANK :]))
    own_q = own_columns(expand_qo[:, :RANK])
    fold = groups == 2 and own_q.shape[2] % LANES == 0
    if fold:
        own_kv = lax.dynamic_slice_in_dim(expand_kv, g * RANK, RANK, 1)
        folds = own_q.shape[2] // own_kv.shape[2]
        own_kv = jnp.concatenate(jnp.split(own_kv, folds, axis=1), axis=2)
        own_q = jnp.concatenate([own_q, own_kv], axis=1)
    else:
        b_kv = along_h(own_columns(expand_kv))
    own_q, sent_y = lax.optimization_barrier((own_q, sent_y))
    b_q = along_h(own_q)

    sent_x, sent_y = lax.optimization_barrier((sent_x, sent_y))

    group_ids = sent_x[:, tok_rows, :tok_rows].astype(jnp.int32)
    near_ids = lax.dynamic_slice_in_dim(group_ids, h * inner, inner, 0)
    group_ids = group_ids.reshape(devices * tok_rows, 1)
    part = shrink(group_ids, sent_x, shrink_panels, 3 * RANK, inner, tok_rows)
    part, near_ids = lax.optimization_barrier((part, near_ids))
    near = jnp.sum(exchange(part, "r").astype(jnp.float32), axis=0).astype(jnp.bfloat16)

    if groups == 2:
        far_ids = lax.ppermute(near_ids, "groups", [(0, 1), (1, 0)])
        first, second = jnp.where(g == 0, near_ids, far_ids), jnp.where(g == 0, far_ids, near_ids)
        plane_ids = jnp.concatenate([first, second], axis=0)
    else:
        plane_ids = lax.all_gather(near_ids, "groups", axis=0, tiled=True)
    swap_ids = plane_ids[p ^ jnp.arange(members)].reshape(rows, 1)
    plane_ids = plane_ids.reshape(rows, 1)
    parts_o = shrink_parts(swap_ids, sent_y, a_o, RANK)
    near, parts_o = lax.optimization_barrier((near, parts_o))
    far = exchange(near, "h")
    parts_o = swap_parts(parts_o)
    low_o = sum(piece.astype(jnp.float32) for piece in parts_o).astype(jnp.bfloat16)
    low = jnp.sum(far.astype(jnp.float32), axis=0).astype(jnp.bfloat16)
    low, own_o = lax.optimization_barrier((low, own_columns(expand_qo[:, RANK:])))
    b_o = along_h(own_o)
    low = jnp.concatenate([low, low_o], axis=1)
    low = lax.all_gather(low, PLANE, axis=0, tiled=True)
    low_all = low.reshape(members, tok_rows, -1)

    def home(low_part, panels):
        full = expand(plane_ids, low_part, panels, tile)
        return exchange(full.reshape(members, tok_rows, -1), PLANE)

    if fold:
        full = expand_joint(g.reshape(1), plane_ids, low, b_q, 0, tile)
        full, low_all = lax.optimization_barrier((full, low_all))
        parts = exchange(full.reshape(members, tok_rows, -1), PLANE)
        narrow = expand_kv.shape[2]
        delta_q, delta_k, delta_v = unpack_joint(parts, narrow, count, inner, groups)
        return delta_q, delta_k, delta_v, finish_o(low_all, b_o)
    low_k, low_v = low[:, RANK : 2 * RANK], low[:, 2 * RANK : 3 * RANK]
    delta_k = unpack(home(low_k, b_kv[:, :, :RANK]), count, inner, groups)
    delta_v = unpack(home(low_v, b_kv[:, :, RANK:]), count, inner, groups)
    delta_q = unpack(home(low[:, :RANK], b_q), count, inner, groups)
    return delta_q, delta_k, delta_v, finish_o(low_all, b_o)


def solution(mesh):
    groups, devices = mesh.devices.shape
    inner = max(SET // groups, 1)
    cut = Mesh(mesh.devices.reshape(groups, devices // inner, inner), ("groups", "h", "r"))
    by_token = P(("groups", "h", "r"))
    by_token_rows = P(("groups", "h", "r"), None)
    by_column = P(None, None, ("h", "r"))
    in_specs = (
        (by_token_rows,) * 2 + (by_token,) * 3 + (P("groups", None),) + (by_column,) * 3
    )
    out_specs = (by_token_rows,) * 4
    return jax.shard_map(shards, mesh=cut, in_specs=in_specs, out_specs=out_specs, check_vma=False)
```

```python
import functools

import jax
import jax.numpy as jnp
from jax import lax
from jax.experimental import pallas as pl
from jax.experimental.pallas import tpu as pltpu
from jax.sharding import Mesh, PartitionSpec as P

LANES = 128
CHUNK = 48
SET = 8
RANK = 64
SCALE = 2.0
VMEM_LIMIT = 48 * 1024 * 1024
PLANE = ("groups", "r")
REQ = ("h", "r")


def call(kernel, name, out_shape, flops, traffic, **kwargs):
    return pl.pallas_call(
        kernel,
        out_shape=out_shape,
        compiler_params=pltpu.CompilerParams(vmem_limit_bytes=VMEM_LIMIT),
        cost_estimate=pl.CostEstimate(flops=flops, bytes_accessed=traffic, transcendentals=0),
        name=name,
        **kwargs,
    )


def bf16(*shape):
    return jax.ShapeDtypeStruct(shape, jnp.bfloat16)


def nt_dot(left, right):
    return lax.dot_general(
        left, right, (((1,), (1,)), ((), ())), preferred_element_type=jnp.float32
    )


def shrink_rows(ids, tokens, panel_of, adapters, ranks):
    pair_of = ids >> 1
    wide = jnp.zeros((ids.shape[0], 2 * ranks), jnp.float32)
    for first in range(0, adapters, 4):
        part = None
        for tokens_piece, panel in zip(tokens, panel_of(first)):
            term = nt_dot(tokens_piece, panel.reshape(4 * ranks, panel.shape[2]))
            part = term if part is None else part + term
        for j in range(2):
            at = 2 * j * ranks
            wide = jnp.where(pair_of == first // 2 + j, part[:, at : at + 2 * ranks], wide)
    return jnp.where((ids & 1) == 1, wide[:, ranks:], wide[:, :ranks])


def shrink_kernel(ranks, ids_ref, tokens_ref, panel_ref, out_ref):
    sources, rows = out_ref.shape[0], out_ref.shape[2]
    tokens = tokens_ref[:, :rows, :].reshape(sources * rows, tokens_ref.shape[2])
    low = shrink_rows(
        ids_ref[...],
        [tokens],
        lambda first: [panel_ref[first : first + 4, :ranks]],
        panel_ref.shape[0],
        ranks,
    )
    out_ref[...] = low.astype(out_ref.dtype).reshape(out_ref.shape)


def shrink(ids, tokens, panels, ranks, inner, tok_rows):
    sources, held_rows, columns = tokens.shape
    adapters, held, _ = panels.shape
    tile = inner * tok_rows
    steps = sources // inner
    return call(
        functools.partial(shrink_kernel, ranks),
        "shrink",
        bf16(inner, steps, tok_rows, ranks),
        2 * steps * tile * columns * ranks * adapters,
        2 * (steps * tile + adapters * held) * columns,
        grid=(steps,),
        in_specs=[
            pl.BlockSpec((tile, 1), lambda i: (i, 0)),
            pl.BlockSpec((inner, held_rows, columns), lambda i: (i, 0, 0)),
            pl.BlockSpec((adapters, held, columns), lambda i: (0, 0, 0)),
        ],
        out_specs=pl.BlockSpec((inner, 1, tok_rows, ranks), lambda i: (0, i, 0, 0)),
    )(ids, tokens, panels)


def shrink_parts_kernel(ids_ref, panel_ref, *refs):
    pieces, adapters, _, width = panel_ref.shape
    adapters -= 1
    ranks = refs[-1].shape[1]
    members = len(refs) // 2
    rows = refs[0].shape[0]
    for s in range(0, members, 2):
        both = jnp.concatenate([refs[s][...], refs[s + 1][...]], axis=0)
        low = shrink_rows(
            ids_ref[s * rows : (s + 2) * rows],
            [both[:, k * width : (k + 1) * width] for k in range(pieces)],
            lambda first: [panel_ref[k, first : first + 4, :ranks] for k in range(pieces)],
            adapters,
            ranks,
        ).astype(jnp.bfloat16)
        refs[members + s][...] = low[:rows]
        refs[members + s + 1][...] = low[rows:]


def shrink_parts(ids, tokens, panels, ranks):
    members, (rows, columns) = len(tokens), tokens[0].shape
    adapters = panels.shape[1]
    vmem = pl.BlockSpec(memory_space=pltpu.VMEM)
    return call(
        shrink_parts_kernel,
        "shrink_parts",
        [bf16(rows, ranks)] * members,
        2 * members * rows * columns * ranks * adapters,
        2 * (members * rows + adapters * ranks) * columns,
        in_specs=[vmem] * (2 + members),
        out_specs=[vmem] * members,
    )(ids, panels, *tokens)


def spread_rows(ids, low, adapters):
    spread = jnp.concatenate([low] * adapters, axis=1)
    lane_adapter = lax.broadcasted_iota(jnp.int32, spread.shape, 1) // low.shape[1]
    return jnp.where(lane_adapter == ids, spread, jnp.zeros_like(spread))


def expand_kernel(ids_ref, low_ref, panel_ref, out_ref):
    pieces, adapters, _, width = panel_ref.shape
    ranks = low_ref.shape[1]
    spread = spread_rows(ids_ref[...], low_ref[...], adapters)
    for k in range(pieces):
        panel = panel_ref[k, :, :ranks].reshape(adapters * ranks, width)
        full = jnp.dot(spread, panel, preferred_element_type=jnp.float32)
        out_ref[:, k * width : (k + 1) * width] = (SCALE * full).astype(out_ref.dtype)


def expand(ids, low, panels, tile):
    rows, ranks = low.shape
    pieces, adapters, _, width = panels.shape
    columns = width * pieces
    return call(
        expand_kernel,
        "expand",
        bf16(rows, columns),
        2 * rows * columns * ranks * adapters,
        2 * (rows + adapters * ranks) * columns,
        grid=(rows // tile,),
        in_specs=[
            pl.BlockSpec((tile, 1), lambda i: (i, 0)),
            pl.BlockSpec((tile, ranks), lambda i: (i, 0)),
            pl.BlockSpec(panels.shape, lambda i: (0, 0, 0, 0)),
        ],
        out_specs=pl.BlockSpec((tile, columns), lambda i: (i, 0)),
    )(ids, low, panels)


def expand_joint_kernel(start, g_ref, ids_ref, low_ref, panel_ref, out_ref):
    pieces, adapters, held, width = panel_ref.shape
    ranks = low_ref.shape[1] // 4
    stop = start + ranks
    rows = held - stop
    narrow = rows * width // ranks
    ids = ids_ref[...]
    spread = spread_rows(ids, low_ref[:, :ranks], adapters)
    for k in range(pieces):
        panel = panel_ref[k, :, start:stop].reshape(adapters * ranks, width)
        full = jnp.dot(spread, panel, preferred_element_type=jnp.float32)
        out_ref[:, k * width : (k + 1) * width] = (SCALE * full).astype(out_ref.dtype)
    low_kv = [low_ref[:, j * ranks : (j + 1) * ranks] for j in (1, 2)]
    low_kv = jnp.where(g_ref[0] == 0, *low_kv)
    spread = spread_rows(ids, low_kv, adapters)
    wide = []
    for k in range(pieces):
        parts = [
            panel_ref[k, :, stop:, j * narrow : (j + 1) * narrow]
            for j in range(ranks // rows)
        ]
        wide.append(jnp.concatenate(parts, axis=1))
    panel = jnp.concatenate(wide, axis=2).reshape(adapters * ranks, pieces * narrow)
    full = jnp.dot(spread, panel, preferred_element_type=jnp.float32)
    out_ref[:, pieces * width :] = (SCALE * full).astype(out_ref.dtype)


def expand_joint(g, ids, low, panels, start, tile):
    rows, ranks = low.shape[0], low.shape[1] // 4
    pieces, adapters, held, width = panels.shape
    columns = pieces * (width + (held - start - ranks) * width // ranks)
    return call(
        functools.partial(expand_joint_kernel, start),
        "expand_joint",
        bf16(rows, columns),
        2 * rows * columns * ranks * adapters,
        2 * (rows + adapters * ranks) * columns,
        grid=(rows // tile,),
        in_specs=[
            pl.BlockSpec(memory_space=pltpu.SMEM),
            pl.BlockSpec((tile, 1), lambda i: (i, 0)),
            pl.BlockSpec((tile, 4 * ranks), lambda i: (i, 0)),
            pl.BlockSpec(panels.shape, lambda i: (0, 0, 0, 0)),
        ],
        out_specs=pl.BlockSpec((tile, columns), lambda i: (i, 0)),
    )(g, ids, low, panels)


def expand_parts_kernel(p_ref, ids_ref, low_ref, panel_ref, *out_refs):
    pieces, adapters, ranks, width = panel_ref.shape
    rows, start = low_ref.shape[1], low_ref.shape[2] - ranks
    for s in range(0, len(out_refs), 2):
        pair = [low_ref[p_ref[0] ^ (s + j), :, start:] for j in range(2)]
        spread = spread_rows(
            ids_ref[s * rows : (s + 2) * rows], jnp.concatenate(pair, axis=0), adapters
        )
        for k in range(pieces):
            panel = panel_ref[k].reshape(adapters * ranks, width)
            full = jnp.dot(spread, panel, preferred_element_type=jnp.float32)
            full = (SCALE * full).astype(jnp.bfloat16)
            out_refs[s][:, k * width : (k + 1) * width] = full[:rows]
            out_refs[s + 1][:, k * width : (k + 1) * width] = full[rows:]


def expand_parts(p, ids, low, panels):
    members, rows, _ = low.shape
    pieces, adapters, ranks, width = panels.shape
    columns = pieces * width
    vmem = pl.BlockSpec(memory_space=pltpu.VMEM)
    return call(
        expand_parts_kernel,
        "expand_parts",
        [bf16(rows, columns)] * members,
        2 * members * rows * columns * ranks * adapters,
        2 * (members * rows + adapters * ranks) * columns,
        in_specs=[pl.BlockSpec(memory_space=pltpu.SMEM)] + [vmem] * 3,
        out_specs=[vmem] * members,
    )(p, ids, low, panels)


def exchange(array, axes):
    return lax.all_to_all(array, axes, split_axis=0, concat_axis=0, tiled=True)


def swap_parts(parts):
    members = len(parts)
    return [parts[0]] + [
        lax.ppermute(parts[s], PLANE, [(d, d ^ s) for d in range(members)])
        for s in range(1, members)
    ]


def along_h(array):
    pieces = lax.all_gather(array, "h", axis=0)
    if array.shape[2] % LANES == 0:
        return pieces
    return pieces.transpose(1, 2, 0, 3).reshape((1,) + array.shape[:2] + (-1,))


def piece_places(member, count, inner, groups):
    g, r = member // inner, member % inner
    return [(k * inner + r) * groups + g for k in range(count)]


def window(place, width):
    start = place * width
    return pl.ds(start if isinstance(start, int) else pl.multiple_of(start, width), width)


def pack_parts_kernel(count, inner, groups, p_ref, source_ref, *out_refs):
    width = out_refs[0].shape[1] // count
    for s, out_ref in enumerate(out_refs):
        places = piece_places(p_ref[0] ^ s, count, inner, groups)
        for k, place in enumerate(places):
            out_ref[:, k * width : (k + 1) * width] = source_ref[:, window(place, width)]


def pack_parts(array, p, count, inner, groups):
    rows, columns = array.shape
    members = groups * inner
    width = columns // (count * members)
    if width % LANES:
        cut = array.reshape(rows, count, inner, groups, width).transpose(3, 2, 0, 1, 4)
        cut = cut.reshape(members, rows, count * width)
        return [lax.dynamic_index_in_dim(cut, p[0] ^ s, keepdims=False) for s in range(members)]
    return call(
        functools.partial(pack_parts_kernel, count, inner, groups),
        "pack_parts",
        [bf16(rows, count * width)] * members,
        0,
        4 * rows * columns,
        grid_spec=pltpu.PrefetchScalarGridSpec(
            num_scalar_prefetch=1,
            grid=(rows // CHUNK,),
            in_specs=[pl.BlockSpec((CHUNK, columns), lambda i, p_ref: (i, 0))],
            out_specs=[pl.BlockSpec((CHUNK, count * width), lambda i, p_ref: (i, 0))] * members,
        ),
    )(p, array)


def unpack_parts_kernel(count, inner, groups, p_ref, *refs):
    out_ref = refs[-1]
    width = refs[0].shape[1] // count
    for s, part_ref in enumerate(refs[:-1]):
        places = piece_places(p_ref[0] ^ s, count, inner, groups)
        for k, place in enumerate(places):
            out_ref[:, window(place, width)] = part_ref[:, k * width : (k + 1) * width]


def unpack_parts(parts, p, count, inner, groups):
    members, (rows, columns) = len(parts), parts[0].shape
    if (columns // count) % LANES:
        stacked = jnp.stack(parts)[p[0] ^ jnp.arange(members)]
        return unpack(stacked, count, inner, groups)
    return call(
        functools.partial(unpack_parts_kernel, count, inner, groups),
        "unpack_parts",
        bf16(rows, columns * members),
        0,
        4 * rows * columns * members,
        grid_spec=pltpu.PrefetchScalarGridSpec(
            num_scalar_prefetch=1,
            grid=(rows // CHUNK,),
            in_specs=[pl.BlockSpec((CHUNK, columns), lambda i, p_ref: (i, 0))] * members,
            out_specs=pl.BlockSpec((CHUNK, columns * members), lambda i, p_ref: (i, 0)),
        ),
    )(p, *parts)


def unpack_kernel(count, inner, groups, source_ref, out_ref):
    members, _, columns = source_ref.shape
    width = columns // count
    for m in range(members):
        for k, place in enumerate(piece_places(m, count, inner, groups)):
            out_ref[:, window(place, width)] = source_ref[m, :, k * width : (k + 1) * width]


def unpack(array, count, inner, groups):
    members, rows, columns = array.shape
    width = columns // count
    shape = (rows, columns * members)
    if width % LANES:
        cut = array.reshape(groups, inner, rows, count, width).transpose(2, 3, 1, 0, 4)
        return cut.reshape(shape)
    return call(
        functools.partial(unpack_kernel, count, inner, groups),
        "unpack",
        bf16(*shape),
        0,
        4 * array.size,
        grid=(rows // CHUNK,),
        in_specs=[pl.BlockSpec((members, CHUNK, columns), lambda i: (0, i, 0))],
        out_specs=pl.BlockSpec((CHUNK, columns * members), lambda i: (i, 0)),
    )(array)


def pack_kernel(source_ref, out_ref):
    members, _, width = out_ref.shape
    for m in range(members):
        out_ref[m] = source_ref[:, m * width : (m + 1) * width]


def pack(array, members):
    rows, columns = array.shape
    width = columns // members
    return call(
        pack_kernel,
        "pack",
        bf16(members, rows, width),
        0,
        4 * array.size,
        grid=(rows // CHUNK,),
        in_specs=[pl.BlockSpec((CHUNK, columns), lambda i: (i, 0))],
        out_specs=pl.BlockSpec((members, CHUNK, width), lambda i: (0, i, 0)),
    )(array)


def unpack_joint_kernel(count, inner, groups, narrow, parts_ref, q_ref, k_ref, v_ref):
    members, _, columns = parts_ref.shape
    width = columns // count - narrow
    for m in range(members):
        for k, place in enumerate(piece_places(m, count, inner, groups)):
            q_ref[:, window(place, width)] = parts_ref[m, :, k * width : (k + 1) * width]
    for start, out_ref in ((0, k_ref), (inner, v_ref)):
        for h in range(count):
            for r in range(0, inner, 2):
                at = count * width + h * narrow
                pair = [parts_ref[start + r + j, :, at : at + narrow] for j in range(2)]
                at = (h * inner + r) * narrow
                out_ref[:, at : at + 2 * narrow] = jnp.concatenate(pair, axis=1)


def unpack_joint(parts, narrow, count, inner, groups):
    members, rows, columns = parts.shape
    q_columns = (columns - count * narrow) * members
    kv_columns = count * inner * narrow
    return call(
        functools.partial(unpack_joint_kernel, count, inner, groups, narrow),
        "unpack_joint",
        (bf16(rows, q_columns), bf16(rows, kv_columns), bf16(rows, kv_columns)),
        0,
        4 * parts.size,
        grid=(rows // CHUNK,),
        in_specs=[pl.BlockSpec((members, CHUNK, columns), lambda i: (0, i, 0))],
        out_specs=[
            pl.BlockSpec((CHUNK, q_columns), lambda i: (i, 0)),
            pl.BlockSpec((CHUNK, kv_columns), lambda i: (i, 0)),
            pl.BlockSpec((CHUNK, kv_columns), lambda i: (i, 0)),
        ],
    )(parts)


def shards(
    normed_hidden,
    attn_mixed,
    adapter_ids,
    send_slot,
    padded_row,
    fetch_list,
    shrink_panels,
    expand_qo,
    expand_kv,
):
    groups, count, inner = (lax.axis_size(a) for a in ("groups", "h", "r"))
    g, h, r = (lax.axis_index(a) for a in ("groups", "h", "r"))
    p = (g * inner + r).reshape(1)
    devices = count * inner
    members = groups * inner
    tok_rows = normed_hidden.shape[0]
    slot_rows = 2 * tok_rows // devices
    rows = members * tok_rows
    tile = 2 * tok_rows

    def own_columns(panel):
        width = panel.shape[2] // groups
        return lax.dynamic_slice_in_dim(panel, g * width, width, 2)

    def finish_o(low_o, b_o):
        full_o = expand_parts(p, swap_ids, low_o, b_o)
        return unpack_parts(swap_parts(full_o), p, count, inner, groups)

    owner = send_slot // slot_rows
    at_owner = owner[:, None] == jnp.arange(devices)[None, :]
    listed = jnp.any(fetch_list[None] == adapter_ids[:, None, None], axis=2)
    own_ids = jnp.where(jnp.any(at_owner & listed, axis=1), adapter_ids, -1)
    packed_x = pack(normed_hidden, devices)
    sent_x = exchange(packed_x, REQ)

    attn_mixed, packed_x = lax.optimization_barrier((attn_mixed, packed_x))
    sent_y = swap_parts(pack_parts(attn_mixed, p, count, inner, groups))
    own_ids, packed_x = lax.optimization_barrier((own_ids, packed_x))
    plane_ids = lax.all_gather(own_ids[None], PLANE, axis=0, tiled=True)
    near_ids = lax.dynamic_slice_in_dim(plane_ids, g * inner, inner, 0)
    own_a = own_columns(shrink_panels[:, 3 * RANK :])
    note = near_ids.astype(jnp.bfloat16)
    note = jnp.pad(note, ((0, 0), (0, -tok_rows % own_a.shape[2])))
    note = note.reshape(1, -1, own_a.shape[2])
    note_rows = note.shape[1]
    note = jnp.pad(note, ((0, 0), (0, RANK - note_rows), (0, 0)))
    gathered = lax.all_gather(jnp.concatenate([own_a, note], axis=0), "h", axis=0)
    group_ids = gathered[:, -1, :note_rows].reshape(count, inner, -1)[:, :, :tok_rows]
    group_ids = group_ids.astype(jnp.int32).reshape(devices * tok_rows, 1)
    a_o = gathered
    if own_a.shape[2] % LANES:
        a_o = gathered.transpose(1, 2, 0, 3).reshape((1,) + gathered.shape[1:3] + (-1,))
    own_q = own_columns(expand_qo[:, :RANK])
    fold = groups == 2 and own_q.shape[2] % LANES == 0
    if fold:
        own_kv = lax.dynamic_slice_in_dim(expand_kv, g * RANK, RANK, 1)
        folds = own_q.shape[2] // own_kv.shape[2]
        own_kv = jnp.concatenate(jnp.split(own_kv, folds, axis=1), axis=2)
        own_q = jnp.concatenate([own_q, own_kv], axis=1)
    else:
        b_kv = along_h(own_columns(expand_kv))
    own_q, sent_y = lax.optimization_barrier((own_q, sent_y))
    b_q = along_h(own_q)

    sent_x, sent_y = lax.optimization_barrier((sent_x, sent_y))

    part = shrink(group_ids, sent_x, shrink_panels, 3 * RANK, inner, tok_rows)
    near = jnp.sum(exchange(part, "r").astype(jnp.float32), axis=0).astype(jnp.bfloat16)

    swap_ids = plane_ids[p ^ jnp.arange(members)].reshape(rows, 1)
    plane_ids = plane_ids.reshape(rows, 1)
    parts_o = shrink_parts(swap_ids, sent_y, a_o, RANK)
    near, parts_o = lax.optimization_barrier((near, parts_o))
    far = exchange(near, "h")
    parts_o = swap_parts(parts_o)
    low_o = sum(piece.astype(jnp.float32) for piece in parts_o).astype(jnp.bfloat16)
    low = jnp.sum(far.astype(jnp.float32), axis=0).astype(jnp.bfloat16)
    low, own_o = lax.optimization_barrier((low, own_columns(expand_qo[:, RANK:])))
    b_o = along_h(own_o)
    low = jnp.concatenate([low, low_o], axis=1)
    low = lax.all_gather(low, PLANE, axis=0, tiled=True)
    low_all = low.reshape(members, tok_rows, -1)

    def home(low_part, panels):
        full = expand(plane_ids, low_part, panels, tile)
        return exchange(full.reshape(members, tok_rows, -1), PLANE)

    if fold:
        full = expand_joint(g.reshape(1), plane_ids, low, b_q, 0, tile)
        full, low_all = lax.optimization_barrier((full, low_all))
        parts = exchange(full.reshape(members, tok_rows, -1), PLANE)
        narrow = expand_kv.shape[2]
        delta_q, delta_k, delta_v = unpack_joint(parts, narrow, count, inner, groups)
        return delta_q, delta_k, delta_v, finish_o(low_all, b_o)
    low_k, low_v = low[:, RANK : 2 * RANK], low[:, 2 * RANK : 3 * RANK]
    delta_k = unpack(home(low_k, b_kv[:, :, :RANK]), count, inner, groups)
    delta_v = unpack(home(low_v, b_kv[:, :, RANK:]), count, inner, groups)
    delta_q = unpack(home(low[:, :RANK], b_q), count, inner, groups)
    return delta_q, delta_k, delta_v, finish_o(low_all, b_o)


def solution(mesh):
    groups, devices = mesh.devices.shape
    inner = max(SET // groups, 1)
    cut = Mesh(mesh.devices.reshape(groups, devices // inner, inner), ("groups", "h", "r"))
    by_token = P(("groups", "h", "r"))
    by_token_rows = P(("groups", "h", "r"), None)
    by_column = P(None, None, ("h", "r"))
    in_specs = (
        (by_token_rows,) * 2 + (by_token,) * 3 + (P("groups", None),) + (by_column,) * 3
    )
    out_specs = (by_token_rows,) * 4
    return jax.shard_map(shards, mesh=cut, in_specs=in_specs, out_specs=out_specs, check_vma=False)
```
